32 devices in a mesh: dp: 8 (over y, x, core), pipe: 4 (over z).
Axes of the slice: x: 2, y: 2, z: 4, core: 2. Of those that a mesh axis runs over, the one named last changes fastest.
Arguments:
- stashed: bfloat16 [4, 4, 256, 8192], P('pipe', None, 'dp'), may hold values from -6 to 6
- kv_grads: bfloat16 [4, 4, 256, 2048], P('pipe', None, 'dp'), may hold values from -0.1875 to 0.1875
- branch_grads: bfloat16 [4, 256, 8192], P('pipe', 'dp'), may hold values from -6 to 6
- flora_seeds: int32 [4, 2], P('pipe'), may hold values from 0 to 99999
- plan: int32 [4, 4], P('pipe'), may hold values from 0 to 3, each once within a row
Outputs:
- compressed: float32 [4, 256, 2048], P('pipe')
- section_grads: bfloat16 [4, 256, 8192], P('pipe', 'dp')
The draws below stay inside these ranges and needn't reach their ends.
Inputs may be any that keep to these rules, and one draw needn't show every extreme that they name: `plan`: each row is a permutation of the micro-batch numbers 0 to 3.
All inputs are finite; a program needn't handle non-finite values.
Results may differ from the reference program's by a relative error of at most 0.0051.
Values may be sent and summed in bfloat16 or wider, within the bound.
No kernel may reach another device: no remote copies, remote signals or barrier semaphores. Data moves between devices by JAX's collectives and lax.ppermute only.
A program may use at most 64 MiB of HBM per device.

```python
import math
import jax
import jax.numpy as jnp

D = 8192
KVW = 1024
R = 256
MBW = 4
TOK_MB = 32
SECTIONS = 4
TOKS = 256
N_DP = 8


def place_ends(drawn, key, smallest, top_value):
    dims = drawn.shape
    index_at = [jax.random.randint(jax.random.fold_in(key, axis), (), 0, dims[axis]) for axis in range(len(dims))]
    drawn = drawn.at[tuple(index_at)].set(smallest)
    longest = dims.index(max(dims))
    index_at[longest] = (index_at[longest] + 1) % dims[longest]
    return drawn.at[tuple(index_at)].set(top_value)


def steps_of(own_key, shape, cuts, least, high):
    factor_of, own = 1.0, jax.random.fold_in(own_key, 6)
    for dim, blocks in cuts:
        heights = jnp.exp(jax.random.uniform(jax.random.fold_in(own, dim), (blocks,), jnp.float32, least / len(cuts), high / len(cuts)))
        factor_of = factor_of * jnp.repeat(heights, shape[dim] // blocks).reshape([-1 if axis == dim else 1 for axis in range(len(shape))])
    return factor_of


def scatter_about(key, dims, scale, most, pieces=(), kind=jnp.bfloat16):
    gain = steps_of(key, dims, pieces, -0.22, 0.18) if pieces else 1.0
    drawn = jax.random.normal(key, dims, jnp.float32) * scale * gain
    return jnp.minimum(jnp.maximum(drawn, -most), most).astype(kind)


def setup_inputs(seed: int = 0) -> dict:
    splits = jax.random.split(jax.random.key(seed), 6)
    return {
        "stashed": scatter_about(splits[0], (SECTIONS, MBW, TOKS, D), 1.0, 6.0, ((0, 4), (2, 8))),
        "kv_grads": scatter_about(splits[1], (SECTIONS, MBW, TOKS, 2 * KVW), (MBW * TOK_MB * N_DP) ** -0.5, 0.1875, ((0, 4), (2, 8))),
        "branch_grads": scatter_about(splits[2], (SECTIONS, TOKS, D), 1.0, 6.0, ((0, 4), (1, 8))),
        "flora_seeds": place_ends(jax.random.randint(splits[3], (SECTIONS, 2), 0, 100000), jax.random.fold_in(splits[3], 1), 0, 99999).astype(jnp.int32),
        "plan": jax.vmap(lambda own: jax.random.permutation(own, MBW))(jax.random.split(splits[4], SECTIONS)).reshape((SECTIONS, MBW)).astype(jnp.int32),
    }


def projection(seed_value, row_count, col_count):
    row_index = jnp.arange(row_count, dtype=jnp.int32)[:, None]
    col_index = jnp.arange(col_count, dtype=jnp.int32)[None, :]
    hashed_one = (row_index * 1031 + col_index * 2053 + seed_value * 3 + 7) % 32749
    hashed_two = (hashed_one * hashed_one + row_index * 17 + 5) % 32749
    hashed_three = (hashed_two * hashed_two + col_index * 29 + seed_value) % 32749
    scaled = hashed_three.astype(jnp.float32) * (2.0 / 32748.0) - 1.0
    return (scaled * math.sqrt(3.0 / row_count)).astype(jnp.bfloat16)

def reference(stashed, kv_grads, branch_grads, flora_seeds, plan):
    outputs = []
    for section_num in range(SECTIONS):
        key_proj = projection(flora_seeds[section_num, 0], D, R)
        value_proj = projection(flora_seeds[section_num, 1], D, R)
        key_total = jnp.zeros((R, KVW), jnp.float32)
        value_total = jnp.zeros((R, KVW), jnp.float32)
        for slot_num in range(MBW):
            inputs = stashed[section_num, slot_num]
            kv_rows = kv_grads[section_num, plan[section_num, slot_num]]
            key_side = jnp.dot(inputs, key_proj, preferred_element_type=jnp.float32).astype(jnp.bfloat16)
            value_side = jnp.dot(inputs, value_proj, preferred_element_type=jnp.float32).astype(jnp.bfloat16)
            key_total = key_total + jnp.dot(key_side.T, kv_rows[:, :KVW], preferred_element_type=jnp.float32)
            value_total = value_total + jnp.dot(value_side.T, kv_rows[:, KVW:], preferred_element_type=jnp.float32)
        outputs.append(jnp.concatenate([key_total, value_total], axis=1))
    compressed = jnp.stack(outputs)
    running = branch_grads[SECTIONS - 1]
    chain_list = [running]
    for section_num in range(SECTIONS - 2, -1, -1):
        running = (running.astype(jnp.float32) + branch_grads[section_num].astype(jnp.float32)).astype(jnp.bfloat16)
        chain_list.append(running)
    section_grads = jnp.stack(chain_list[::-1])
    return (compressed, section_grads)
```

```python
import functools
import math

import jax
import jax.numpy as jnp
import ml_dtypes
import numpy as np
from jax import lax
from jax.experimental import pallas as pl
from jax.experimental.pallas import tpu as pltpu
from jax.sharding import PartitionSpec as P

PRIME = 32749
R = 256
TERMS = 32
CHUNKS = 4
DEPTH = 2


def balanced(values):
    return (values + PRIME // 2) % PRIME - PRIME // 2


def row_digits(rows):
    r = np.arange(rows, dtype=np.int64)
    a = balanced(1031 * r)
    square = balanced(a * a + 17 * r + 5)
    lines = []
    for factor in (balanced(4 * balanced(square * a)), balanced(4 * a * a + 2 * square), balanced(4 * a)):
        for place in range(3):
            rest = np.floor_divide(factor + 16, 32) if place < 2 else 0 * factor
            lines += [factor - 32 * rest] * 2
            factor = rest
    constant = balanced(square * square - PRIME // 2)
    high = np.floor_divide(constant + 128, 256)
    lines += [np.ones_like(r)] * 2 + [256 * high, constant - 256 * high]
    lines += [np.zeros_like(r)] * (TERMS - len(lines))
    return np.stack(lines).astype(ml_dtypes.bfloat16)


def reduced(values):
    quotient = jnp.round(values.astype(jnp.float32) * jnp.float32(1 / PRIME)).astype(jnp.int32)
    return values - quotient * PRIME


def column_digits(seed, columns):
    c = lax.broadcasted_iota(jnp.int32, (columns, 128), 0)
    term = lax.broadcasted_iota(jnp.int32, (columns, 128), 1)
    b = reduced(2053 * c + (3 * seed + 7))
    b2 = reduced(b * b)
    b3 = reduced(b2 * b)
    added = reduced(reduced(b2 * b2) + 29 * c + seed)
    base = jnp.where(term < 6, b, jnp.where(term < 12, b2, jnp.where(term < 18, b3, added)))
    within = jnp.where(term < 6, term, jnp.where(term < 12, term - 6, term - 12))
    place = jnp.where(term >= 18, 1, jnp.where(within < 2, 1, jnp.where(within < 4, 32, 1024)))
    whole = reduced(base * place).astype(jnp.float32)
    high = jnp.round(whole * (1 / 256)) * 256
    digit = jnp.where((term & 1) == 0, high, whole - high)
    digit = jnp.where(term >= 20, jnp.where(term < 22, 1.0, 0.0), digit)
    return digit.astype(jnp.bfloat16)


def compress_kernel(
    tile, groups, scale, halves, axis,
    seeds_hbm, plan_hbm, stash, kv_hbm, digits_hbm, keep, send,
    seeds, plan, x, kv, digits, columns, total, scalar_sem, x_sem, kv_sem, digit_sem,
):
    slots, tokens, width = stash.shape
    scalars = [
        pltpu.make_async_copy(seeds_hbm, seeds, scalar_sem.at[0]),
        pltpu.make_async_copy(plan_hbm, plan, scalar_sem.at[1]),
    ]
    for copy in scalars:
        copy.start()
    digit_copy = pltpu.make_async_copy(digits_hbm, digits, digit_sem)
    digit_copy.start()
    kv_copy = pltpu.make_async_copy(kv_hbm, kv, kv_sem)
    span = width // groups
    for copy in scalars:
        copy.wait()
    copies = [
        [
            pltpu.make_async_copy(
                stash.at[k, :, pl.ds(g * span, span)],
                x.at[plan[0, k], :, pl.ds(g * span, span)],
                x_sem.at[g, k],
            )
            for k in range(slots)
        ]
        for g in range(groups)
    ]
    for group in copies:
        for copy in group:
            copy.start()
    kv_copy.start()
    columns[0:R, :] = column_digits(seeds[0, 0], R)
    columns[R:, :] = column_digits(seeds[0, 1], R)
    digit_copy.wait()
    total[...] = jnp.zeros_like(total)
    for g in range(groups):
        for copy in copies[g]:
            copy.wait()
        for i in range(span // tile):
            part = pl.ds(g * span + i * tile, tile)
            hashed = jnp.dot(columns[:, 0:TERMS], digits[:, part], preferred_element_type=jnp.float32)
            turns = hashed * jnp.float32(1 / PRIME)
            proj = ((turns - jnp.round(turns)) * jnp.float32(scale)).astype(jnp.bfloat16)
            total[...] += lax.dot_general(
                proj, x[:, :, part].reshape(slots * tokens, tile), (((1,), (1,)), ((), ())),
                preferred_element_type=jnp.float32,
            )
    kv_copy.wait()
    half = kv.shape[2] // 2
    targets = kv[...].reshape(slots * tokens, 2 * half)
    rows = R // halves
    mine = lax.rem(lax.axis_index(axis), halves)
    for other, out in enumerate((keep, send)[:halves]):
        at = lax.rem(mine + other, halves) * rows
        for side in range(2):
            left = total[pl.ds(pl.multiple_of(side * R + at, rows), rows), :].astype(jnp.bfloat16)
            cols = slice(side * half, (side + 1) * half)
            out[:, cols] = jnp.dot(left, targets[:, cols], preferred_element_type=jnp.float32).astype(out.dtype)


def compressed_parts(stash, kv, seeds, plan, halves, axis):
    slots, tokens, width = stash.shape
    groups = 4
    tile = width // 16
    scale = PRIME * 2.0 / (PRIME - 1) * math.sqrt(3.0 / width)
    anywhere = pl.BlockSpec(memory_space=pl.ANY)
    digits = jnp.asarray(row_digits(width))
    part = (R // halves, kv.shape[2])
    return pl.pallas_call(
        functools.partial(compress_kernel, tile, groups, scale, halves, axis),
        out_shape=[jax.ShapeDtypeStruct(part, jnp.float32), jax.ShapeDtypeStruct(part, jnp.bfloat16)],
        in_specs=[anywhere] * 5,
        out_specs=[pl.BlockSpec(memory_space=pltpu.VMEM)] * 2,
        scratch_shapes=[
            pltpu.SMEM(seeds.shape, jnp.int32),
            pltpu.SMEM(plan.shape, jnp.int32),
            pltpu.VMEM((slots, tokens, width), jnp.bfloat16),
            pltpu.VMEM(kv.shape, jnp.bfloat16),
            pltpu.VMEM(digits.shape, jnp.bfloat16),
            pltpu.VMEM((2 * R, 128), jnp.bfloat16),
            pltpu.VMEM((2 * R, slots * tokens), jnp.float32),
            pltpu.SemaphoreType.DMA((2,)),
            pltpu.SemaphoreType.DMA((groups, slots)),
            pltpu.SemaphoreType.DMA,
            pltpu.SemaphoreType.DMA,
        ],
        compiler_params=pltpu.CompilerParams(vmem_limit_bytes=48 * 2**20),
        name="compress",
    )(seeds, plan, stash, kv, digits)


def exchanged(value, axis, distance):
    size = lax.axis_size(axis)
    return lax.ppermute(value, axis, [(i, i ^ distance) for i in range(size)])


def split_kernel(axis, keep, got, *outs):
    chips = len(outs)
    rows = keep.shape[0] // chips
    chip = lax.axis_index(axis) // 2
    for step, out in enumerate(outs):
        at = pl.ds(pl.multiple_of((chip ^ step) * rows, rows), rows)
        out[...] = (keep[at, :] + got[at, :].astype(jnp.float32)).astype(out.dtype)


def sum_kernel(*refs):
    *terms, out = refs
    total = terms[0][...]
    for term in terms[1:]:
        total = total + term[...].astype(jnp.float32)
    out[...] = total.astype(out.dtype)


def assemble_kernel(axis, *refs):
    *pieces, out = refs
    chips = len(pieces) // 2
    rows = pieces[0].shape[0]
    device = lax.axis_index(axis)
    for side in range(2):
        core = lax.rem(device, 2) ^ side
        for step in range(chips):
            at = (core * chips + ((device // 2) ^ step)) * rows
            out[pl.ds(pl.multiple_of(at, rows), rows), :] = pieces[side * chips + step][...].astype(out.dtype)


def vmem_call(kernel, outs, name, *args):
    inside = pl.BlockSpec(memory_space=pltpu.VMEM)
    return pl.pallas_call(
        kernel,
        out_shape=outs,
        in_specs=[inside] * len(args),
        out_specs=jax.tree.map(lambda _: inside, outs),
        compiler_params=pltpu.CompilerParams(vmem_limit_bytes=32 * 2**20),
        name=name,
    )(*args)


def summed_over(stash, kv, seeds, plan, axis):
    size = lax.axis_size(axis)
    chips = size // 2
    columns = kv.shape[2]
    small = chips in (1, 2, 4) and size == 2 * chips
    if not small:
        keep, _ = compressed_parts(stash, kv, seeds, plan, 1, axis)
        return lax.psum(keep, axis)
    keep, send = compressed_parts(stash, kv, seeds, plan, 2, axis)
    got = exchanged(send, axis, 1)
    piece = (R // size, columns)
    own, *sends = vmem_call(
        functools.partial(split_kernel, axis),
        [jax.ShapeDtypeStruct(piece, jnp.float32 if s == 0 else jnp.bfloat16) for s in range(chips)],
        "split", keep, got,
    )
    gots = [exchanged(value, axis, 2 * s) for s, value in enumerate(sends, 1)]
    done = vmem_call(sum_kernel, jax.ShapeDtypeStruct(piece, jnp.bfloat16), "sum", own, *gots)
    mine = [done] + [exchanged(done, axis, 2 * s) for s in range(1, chips)]
    theirs = [exchanged(value, axis, 1) for value in mine]
    return vmem_call(
        functools.partial(assemble_kernel, axis), jax.ShapeDtypeStruct((R, columns), jnp.float32),
        "assemble", *mine, *theirs,
    )


def added(a, b):
    return (a.astype(jnp.float32) + b.astype(jnp.float32)).astype(jnp.bfloat16)


def suffix_sums(own, axis):
    size, mine = lax.axis_size(axis), lax.axis_index(axis)
    width = own.shape[1] // CHUNKS
    chunk = [own[:, i * width:(i + 1) * width] for i in range(CHUNKS)]
    pairs = [(i, (i - 1) % size) for i in range(size)]

    def by_place(pick):
        value = pick(0)
        for place in range(1, size):
            value = jnp.where(mine == size - 1 - place, pick(place), value)
        return value

    sums, gots = [], []
    steps = CHUNKS + (size - 1) * DEPTH
    for step in range(steps):
        value = by_place(lambda place: chunk[(step - place * DEPTH) % CHUNKS])
        if step >= DEPTH:
            value = jnp.where(mine == size - 1, value, added(gots[step - DEPTH], value))
        sums.append(value)
        if step < steps - DEPTH:
            gots.append(lax.ppermute(value, axis, pairs))
    return jnp.concatenate(
        [by_place(lambda place: sums[i + place * DEPTH]) for i in range(CHUNKS)], axis=1
    )


def per_device(stashed, kv_grads, branch_grads, flora_seeds, plan):
    compressed = summed_over(stashed[0], kv_grads[0], flora_seeds, plan, "dp")
    running = suffix_sums(branch_grads[0], "pipe")
    return compressed[None], running[None]


def solution(mesh):
    placed = (
        P("pipe", None, "dp", None),
        P("pipe", None, "dp", None),
        P("pipe", "dp", None),
        P("pipe", None),
        P("pipe", None),
    )
    return jax.shard_map(
        per_device,
        mesh=mesh,
        in_specs=placed,
        out_specs=(P("pipe", None, None), P("pipe", "dp", None)),
        check_vma=False,
    )
```

```python
import functools
import math

import jax
import jax.numpy as jnp
import ml_dtypes
import numpy as np
from jax import lax
from jax.experimental import pallas as pl
from jax.experimental.pallas import tpu as pltpu
from jax.sharding import PartitionSpec as P

PRIME = 32749
R = 256
TERMS = 32


def balanced(values):
    return (values + PRIME // 2) % PRIME - PRIME // 2


def row_digits(rows):
    r = np.arange(rows, dtype=np.int64)
    a = balanced(1031 * r)
    square = balanced(a * a + 17 * r + 5)
    lines = []
    for factor in (balanced(4 * balanced(square * a)), balanced(4 * a * a + 2 * square), balanced(4 * a)):
        for place in range(3):
            rest = np.floor_divide(factor + 16, 32) if place < 2 else 0 * factor
            lines += [factor - 32 * rest] * 2
            factor = rest
    constant = balanced(square * square - PRIME // 2)
    high = np.floor_divide(constant + 128, 256)
    lines += [np.ones_like(r)] * 2 + [256 * high, constant - 256 * high]
    lines += [np.zeros_like(r)] * (TERMS - len(lines))
    return np.stack(lines).astype(ml_dtypes.bfloat16)


def reduced(values):
    quotient = jnp.round(values.astype(jnp.float32) * jnp.float32(1 / PRIME)).astype(jnp.int32)
    return values - quotient * PRIME


def column_digits(seed, columns):
    c = lax.broadcasted_iota(jnp.int32, (columns, 128), 0)
    term = lax.broadcasted_iota(jnp.int32, (columns, 128), 1)
    b = reduced(2053 * c + (3 * seed + 7))
    b2 = reduced(b * b)
    b3 = reduced(b2 * b)
    added = reduced(reduced(b2 * b2) + 29 * c + seed)
    base = jnp.where(term < 6, b, jnp.where(term < 12, b2, jnp.where(term < 18, b3, added)))
    within = jnp.where(term < 6, term, jnp.where(term < 12, term - 6, term - 12))
    place = jnp.where(term >= 18, 1, jnp.where(within < 2, 1, jnp.where(within < 4, 32, 1024)))
    whole = reduced(base * place).astype(jnp.float32)
    high = jnp.round(whole * (1 / 256)) * 256
    digit = jnp.where((term & 1) == 0, high, whole - high)
    digit = jnp.where(term >= 20, jnp.where(term < 22, 1.0, 0.0), digit)
    return digit.astype(jnp.bfloat16)


def compress_kernel(
    tile, groups, scale, halves, axis,
    seeds_hbm, plan_hbm, stash, kv_hbm, digits_hbm, kept, send,
    seeds, plan, x, kv, digits, columns, total, scalar_sem, x_sem, kv_sem, digit_sem,
):
    slots, tokens, width = stash.shape
    span = width // groups
    scalars = [
        pltpu.make_async_copy(seeds_hbm, seeds, scalar_sem.at[0]),
        pltpu.make_async_copy(plan_hbm, plan, scalar_sem.at[1]),
    ]
    digit_copy = pltpu.make_async_copy(digits_hbm, digits, digit_sem)
    copies = [
        pltpu.make_async_copy(
            stash.at[:, :, pl.ds(g * span, span)], x.at[:, :, pl.ds(g * span, span)], x_sem.at[g]
        )
        for g in range(groups)
    ]
    for copy in (*scalars, digit_copy, *copies):
        copy.start()
    for copy in scalars:
        copy.wait()
    kv_copies = [
        pltpu.make_async_copy(kv_hbm.at[plan[0, k]], kv.at[k], kv_sem.at[k]) for k in range(slots)
    ]
    for copy in kv_copies:
        copy.start()
    columns[0:R, :] = column_digits(seeds[0, 0], R)
    columns[R:, :] = column_digits(seeds[0, 1], R)
    digit_copy.wait()
    total[...] = jnp.zeros_like(total)
    for g in range(groups):
        copies[g].wait()
        for i in range(span // tile):
            part = pl.ds(g * span + i * tile, tile)
            hashed = jnp.dot(columns[:, 0:TERMS], digits[:, part], preferred_element_type=jnp.float32)
            turns = hashed * jnp.float32(1 / PRIME)
            proj = ((turns - jnp.round(turns)) * jnp.float32(scale)).astype(jnp.bfloat16)
            total[...] += lax.dot_general(
                proj, x[:, :, part].reshape(slots * tokens, tile), (((1,), (1,)), ((), ())),
                preferred_element_type=jnp.float32,
            )
    for copy in kv_copies:
        copy.wait()
    half = kv.shape[2] // 2
    targets = kv[...].reshape(slots * tokens, 2 * half)
    rows = R // halves
    mine = lax.rem(lax.axis_index(axis), halves)
    for side in range(2):
        kept[side] = total[pl.ds(pl.multiple_of(side * R + mine * rows, rows), rows), :].astype(jnp.bfloat16)
        if halves > 1:
            other = pl.multiple_of(side * R + (1 - mine) * rows, rows)
            left = total[pl.ds(other, rows), :].astype(jnp.bfloat16)
            cols = slice(side * half, (side + 1) * half)
            send[:, cols] = jnp.dot(
                left, targets[:, cols], preferred_element_type=jnp.float32
            ).astype(send.dtype)


def keep_kernel(plan_hbm, kv_hbm, kept, out, plan, kv, plan_sem, kv_sem):
    slots, tokens, width = kv.shape
    plan_copy = pltpu.make_async_copy(plan_hbm, plan, plan_sem)
    plan_copy.start()
    plan_copy.wait()
    copies = [pltpu.make_async_copy(kv_hbm.at[plan[0, k]], kv.at[k], kv_sem.at[k]) for k in range(slots)]
    for copy in copies:
        copy.start()
    for copy in copies:
        copy.wait()
    targets = kv[...].reshape(slots * tokens, width)
    for side in range(2):
        cols = slice(side * width // 2, (side + 1) * width // 2)
        out[:, cols] = jnp.dot(kept[side], targets[:, cols], preferred_element_type=jnp.float32)


def kept_part(plan, kv, kept):
    inside, far = pl.BlockSpec(memory_space=pltpu.VMEM), pl.BlockSpec(memory_space=pl.ANY)
    return pl.pallas_call(
        keep_kernel,
        out_shape=jax.ShapeDtypeStruct((kept.shape[1], kv.shape[2]), jnp.float32),
        in_specs=[far, far, inside],
        out_specs=inside,
        scratch_shapes=[
            pltpu.SMEM(plan.shape, jnp.int32),
            pltpu.VMEM(kv.shape, jnp.bfloat16),
            pltpu.SemaphoreType.DMA,
            pltpu.SemaphoreType.DMA((kv.shape[0],)),
        ],
        compiler_params=pltpu.CompilerParams(vmem_limit_bytes=16 * 2**20),
        cost_estimate=pl.CostEstimate(flops=10**9, bytes_accessed=4 * 10**6, transcendentals=0),
        name="keep",
    )(plan, kv, kept)


def compressed_parts(stash, kv, seeds, plan, halves, axis):
    slots, tokens, width = stash.shape
    groups = 4
    tile = width // 16
    scale = PRIME * 2.0 / (PRIME - 1) * math.sqrt(3.0 / width)
    far = pl.BlockSpec(memory_space=pl.ANY)
    digits = jnp.asarray(row_digits(width))
    part = (R // halves, kv.shape[2])
    sides = (2, R // halves, slots * tokens)
    return pl.pallas_call(
        functools.partial(compress_kernel, tile, groups, scale, halves, axis),
        out_shape=[jax.ShapeDtypeStruct(sides, jnp.bfloat16), jax.ShapeDtypeStruct(part, jnp.bfloat16)],
        in_specs=[far] * 5,
        out_specs=[pl.BlockSpec(memory_space=pltpu.VMEM)] * 2,
        scratch_shapes=[
            pltpu.SMEM(seeds.shape, jnp.int32),
            pltpu.SMEM(plan.shape, jnp.int32),
            pltpu.VMEM((slots, tokens, width), jnp.bfloat16),
            pltpu.VMEM(kv.shape, jnp.bfloat16),
            pltpu.VMEM(digits.shape, jnp.bfloat16),
            pltpu.VMEM((2 * R, 128), jnp.bfloat16),
            pltpu.VMEM((2 * R, slots * tokens), jnp.float32),
            pltpu.SemaphoreType.DMA((2,)),
            pltpu.SemaphoreType.DMA((groups,)),
            pltpu.SemaphoreType.DMA((slots,)),
            pltpu.SemaphoreType.DMA,
        ],
        compiler_params=pltpu.CompilerParams(vmem_limit_bytes=60 * 2**20),
        cost_estimate=pl.CostEstimate(flops=8 * 10**9, bytes_accessed=28 * 10**6, transcendentals=0),
        name="compress",
    )(seeds, plan, stash, kv, digits)


def exchanged(value, axis, distance):
    size = lax.axis_size(axis)
    return lax.ppermute(value, axis, [(i, i ^ distance) for i in range(size)])


def split_kernel(axis, keep, got, *outs):
    chips = len(outs)
    rows = keep.shape[0] // chips
    chip = lax.axis_index(axis) // 2
    for step, out in enumerate(outs):
        at = pl.ds(pl.multiple_of((chip ^ step) * rows, rows), rows)
        out[...] = (keep[at, :] + got[at, :].astype(jnp.float32)).astype(out.dtype)


def sum_kernel(*refs):
    *terms, out = refs
    total = terms[0][...]
    for term in terms[1:]:
        total = total + term[...].astype(jnp.float32)
    out[...] = total.astype(out.dtype)


def assemble_kernel(axis, *refs):
    *pieces, out = refs
    chips = len(pieces) // 2
    rows = pieces[0].shape[0]
    device = lax.axis_index(axis)
    for side in range(2):
        core = lax.rem(device, 2) ^ side
        for step in range(chips):
            at = (core * chips + ((device // 2) ^ step)) * rows
            out[pl.ds(pl.multiple_of(at, rows), rows), :] = pieces[side * chips + step][...].astype(out.dtype)


def vmem_call(kernel, outs, name, *args, after=(), cost=None):
    inside, anywhere = pl.BlockSpec(memory_space=pltpu.VMEM), pl.BlockSpec(memory_space=pl.ANY)

    def body(*refs):
        kernel(*refs[:len(args)], *refs[len(args) + len(after):])

    return pl.pallas_call(
        body,
        out_shape=outs,
        in_specs=[inside] * len(args) + [anywhere] * len(after),
        out_specs=jax.tree.map(lambda _: inside, outs),
        compiler_params=pltpu.CompilerParams(vmem_limit_bytes=32 * 2**20),
        cost_estimate=cost,
        name=name,
    )(*args, *after)


def add_kernel(a, b, out):
    out[...] = (a[...].astype(jnp.float32) + b[...].astype(jnp.float32)).astype(out.dtype)


def add_after(a, b, *after):
    return vmem_call(add_kernel, jax.ShapeDtypeStruct(a.shape, a.dtype), "add", a, b, after=after)


def added(a, b):
    return (a.astype(jnp.float32) + b.astype(jnp.float32)).astype(jnp.bfloat16)


def between_places(value, swaps, axis, other_axis):
    size, others = lax.axis_size(axis), lax.axis_size(other_axis)
    goes = dict(swaps) | {b: a for a, b in swaps}
    pairs = [
        (i * size + place, i * size + goes[place] if place in goes else (i ^ 1) * size + place)
        for place in range(size)
        for i in range(others)
    ]
    return lax.ppermute(value, (other_axis, axis), pairs)


def chain(own, axis):
    size, mine = lax.axis_size(axis), lax.axis_index(axis)
    value = own
    for place in range(size - 1, 0, -1):
        got = lax.ppermute(value, axis, [(place, place - 1)])
        value = jnp.where(mine == place - 1, added(got, own), value)
    return value


def per_device(stashed, kv_grads, branch_grads, flora_seeds, plan):
    stash, kv, branch = stashed[0], kv_grads[0], branch_grads[0]
    size = lax.axis_size("dp")
    chips = size // 2
    columns = kv.shape[2]
    if size != 2 * chips or chips not in (1, 2, 4) or lax.axis_size("pipe") != 4:
        kept, _ = compressed_parts(stash, kv, flora_seeds, plan, 1, "dp")
        return lax.psum(kept_part(plan, kv, kept), "dp")[None], chain(branch, "pipe")[None]

    mine = lax.axis_index("pipe")
    rows = branch.shape[0] // 2
    first, second = branch[:rows], branch[rows:]
    pairwise, middle, across = ((3, 2), (1, 0)), ((2, 1),), ((2, 0),)

    def moved(value, swaps):
        return between_places(value, swaps, "pipe", "dp")

    first_a = moved(first, pairwise)
    second_a = moved(second, pairwise)
    kept, send = compressed_parts(stash, kv, flora_seeds, plan, 2, "dp")
    got = exchanged(send, "dp", 1)
    keep = kept_part(plan, kv, kept)
    first_2 = added(first_a, first)
    first_b = moved(first_2, middle)

    piece = (R // size, columns)
    own, *sends = vmem_call(
        functools.partial(split_kernel, "dp"),
        [jax.ShapeDtypeStruct(piece, jnp.float32 if s == 0 else jnp.bfloat16) for s in range(chips)],
        "split", keep, got,
    )
    gots = [exchanged(value, "dp", 2 * s) for s, value in enumerate(sends, 1)]

    second_2 = add_after(second_a, second, keep)
    second_b = moved(second_2, middle)
    second_d = moved(second_2, across)

    done = vmem_call(sum_kernel, jax.ShapeDtypeStruct(piece, jnp.bfloat16), "sum", own, *gots, )
    first_1 = add_after(first_b, first, done)
    first_c = moved(first_1, pairwise)
    here = [done] + [exchanged(done, "dp", 2 * s) for s in range(1, chips)]
    there = [exchanged(value, "dp", 1) for value in here]
    def by_place(values):
        out = values[3]
        for place in range(3):
            out = jnp.where(mine == place, values[place], out)
        return out

    running = jnp.concatenate([
        by_place([added(first_c, first), first_1, first_2, first]),
        by_place([added(added(second_d, second_a), second), added(second_b, second), second_2, second]),
    ])
    compressed = vmem_call(
        functools.partial(assemble_kernel, "dp"), jax.ShapeDtypeStruct((R, columns), jnp.float32),
        "assemble", *here, *there, after=[],
    )

    return compressed[None], running[None]


def solution(mesh):
    placed = (
        P("pipe", None, "dp", None),
        P("pipe", None, "dp", None),
        P("pipe", "dp", None),
        P("pipe", None),
        P("pipe", None),
    )
    return jax.shard_map(
        per_device,
        mesh=mesh,
        in_specs=placed,
        out_specs=(P("pipe", None, None), P("pipe", "dp", None)),
        check_vma=False,
    )
```

```python
import functools
import math

import jax
import jax.numpy as jnp
import ml_dtypes
import numpy as np
from jax import lax
from jax.experimental import pallas as pl
from jax.experimental.pallas import tpu as pltpu
from jax.sharding import PartitionSpec as P

PRIME = 32749
R = 256
TERMS = 32


def balanced(values):
    return (values + PRIME // 2) % PRIME - PRIME // 2


def row_digits(rows):
    r = np.arange(rows, dtype=np.int64)
    a = balanced(1031 * r)
    square = balanced(a * a + 17 * r + 5)
    lines = []
    for factor in (balanced(4 * balanced(square * a)), balanced(4 * a * a + 2 * square), balanced(4 * a)):
        for place in range(3):
            rest = np.floor_divide(factor + 16, 32) if place < 2 else 0 * factor
            lines += [factor - 32 * rest] * 2
            factor = rest
    constant = balanced(square * square - PRIME // 2)
    high = np.floor_divide(constant + 128, 256)
    lines += [np.ones_like(r)] * 2 + [256 * high, constant - 256 * high]
    lines += [np.zeros_like(r)] * (TERMS - len(lines))
    return np.stack(lines).astype(ml_dtypes.bfloat16)


def reduced(values):
    quotient = jnp.round(values.astype(jnp.float32) * jnp.float32(1 / PRIME)).astype(jnp.int32)
    return values - quotient * PRIME


def column_digits(seed, columns):
    c = lax.broadcasted_iota(jnp.int32, (columns, 128), 0)
    term = lax.broadcasted_iota(jnp.int32, (columns, 128), 1)
    b = reduced(2053 * c + (3 * seed + 7))
    b2 = reduced(b * b)
    b3 = reduced(b2 * b)
    added = reduced(reduced(b2 * b2) + 29 * c + seed)
    base = jnp.where(term < 6, b, jnp.where(term < 12, b2, jnp.where(term < 18, b3, added)))
    within = jnp.where(term < 6, term, jnp.where(term < 12, term - 6, term - 12))
    place = jnp.where(term >= 18, 1, jnp.where(within < 2, 1, jnp.where(within < 4, 32, 1024)))
    whole = reduced(base * place).astype(jnp.float32)
    high = jnp.round(whole * (1 / 256)) * 256
    digit = jnp.where((term & 1) == 0, high, whole - high)
    digit = jnp.where(term >= 20, jnp.where(term < 22, 1.0, 0.0), digit)
    return digit.astype(jnp.bfloat16)


def tokens_dot(left, right):
    return lax.dot_general(left, right, (((0,), (0,)), ((), ())), preferred_element_type=jnp.float32)


def compress_kernel(
    tile, groups, scale, halves, axis,
    seeds_hbm, plan_hbm, stash, kv_hbm, digits_hbm, kept, send,
    seeds, plan, x, kv, digits, columns, total, scalar_sem, x_sem, kv_sem, digit_sem,
):
    slots, tokens, width = stash.shape
    span = width // groups
    scalars = [
        pltpu.make_async_copy(seeds_hbm, seeds, scalar_sem.at[0]),
        pltpu.make_async_copy(plan_hbm, plan, scalar_sem.at[1]),
    ]
    digit_copy = pltpu.make_async_copy(digits_hbm, digits, digit_sem)
    copies = [
        pltpu.make_async_copy(
            stash.at[:, :, pl.ds(g * span, span)], x.at[:, :, pl.ds(g * span, span)], x_sem.at[g]
        )
        for g in range(groups)
    ]
    kv_copy = pltpu.make_async_copy(kv_hbm, kv, kv_sem)
    for copy in (*scalars, digit_copy, *copies, kv_copy):
        copy.start()
    for copy in scalars:
        copy.wait()
    columns[0:R, :] = column_digits(seeds[0, 0], R)
    columns[R:, :] = column_digits(seeds[0, 1], R)
    digit_copy.wait()
    total[...] = jnp.zeros_like(total)
    for g in range(groups):
        copies[g].wait()
        for i in range(span // tile):
            part = pl.ds(g * span + i * tile, tile)
            hashed = jnp.dot(columns[:, 0:TERMS], digits[:, part], preferred_element_type=jnp.float32)
            turns = hashed * jnp.float32(1 / PRIME)
            proj = ((turns - jnp.round(turns)) * jnp.float32(scale)).astype(jnp.bfloat16)
            total[...] += lax.dot_general(
                x[:, :, part].reshape(slots * tokens, tile), proj, (((1,), (1,)), ((), ())),
                preferred_element_type=jnp.float32,
            )
    count = slots * tokens
    slot_row = lax.broadcasted_iota(jnp.int32, (count, count), 0)
    place = slot_row
    for k in range(slots):
        within = (slot_row >= k * tokens) & (slot_row < (k + 1) * tokens)
        place = jnp.where(within, slot_row + (plan[0, k] - k) * tokens, place)
    moves = (place == lax.broadcasted_iota(jnp.int32, (count, count), 1)).astype(jnp.bfloat16)
    total[...] = tokens_dot(moves, total[...].astype(jnp.bfloat16))
    kv_copy.wait()
    half = kv.shape[2] // 2
    targets = kv[...].reshape(slots * tokens, 2 * half)
    rows = R // halves
    mine = lax.rem(lax.axis_index(axis), halves)
    for side in range(2):
        kept[side] = total[:, pl.ds(pl.multiple_of(side * R + mine * rows, rows), rows)].astype(jnp.bfloat16)
        if halves > 1:
            other = pl.multiple_of(side * R + (1 - mine) * rows, rows)
            left = total[:, pl.ds(other, rows)].astype(jnp.bfloat16)
            cols = slice(side * half, (side + 1) * half)
            send[:, cols] = tokens_dot(left, targets[:, cols]).astype(send.dtype)


def keep_kernel(kept, kv, out):
    slots, tokens, width = kv.shape
    targets = kv[...].reshape(slots * tokens, width)
    for side in range(2):
        cols = slice(side * width // 2, (side + 1) * width // 2)
        out[:, cols] = tokens_dot(kept[side], targets[:, cols])


def kept_part(kept, kv):
    out = jax.ShapeDtypeStruct((kept.shape[2], kv.shape[2]), jnp.float32)
    return vmem_call(keep_kernel, out, "keep", kept, kv)


def compressed_parts(stash, kv, seeds, plan, halves, axis):
    slots, tokens, width = stash.shape
    groups = 2
    tile = width // 8
    scale = PRIME * 2.0 / (PRIME - 1) * math.sqrt(3.0 / width)
    far = pl.BlockSpec(memory_space=pl.ANY)
    digits = jnp.asarray(row_digits(width))
    part = (R // halves, kv.shape[2])
    sides = (2, slots * tokens, R // halves)
    return pl.pallas_call(
        functools.partial(compress_kernel, tile, groups, scale, halves, axis),
        out_shape=[jax.ShapeDtypeStruct(sides, jnp.bfloat16), jax.ShapeDtypeStruct(part, jnp.bfloat16)],
        in_specs=[far] * 5,
        out_specs=[pl.BlockSpec(memory_space=pltpu.VMEM)] * 2,
        scratch_shapes=[
            pltpu.SMEM(seeds.shape, jnp.int32),
            pltpu.SMEM(plan.shape, jnp.int32),
            pltpu.VMEM((slots, tokens, width), jnp.bfloat16),
            pltpu.VMEM(kv.shape, jnp.bfloat16),
            pltpu.VMEM(digits.shape, jnp.bfloat16),
            pltpu.VMEM((2 * R, 128), jnp.bfloat16),
            pltpu.VMEM((slots * tokens, 2 * R), jnp.float32),
            pltpu.SemaphoreType.DMA((2,)),
            pltpu.SemaphoreType.DMA((groups,)),
            pltpu.SemaphoreType.DMA,
            pltpu.SemaphoreType.DMA,
        ],
        compiler_params=pltpu.CompilerParams(vmem_limit_bytes=60 * 2**20),
        cost_estimate=pl.CostEstimate(flops=8 * 10**9, bytes_accessed=28 * 10**6, transcendentals=0),
        name="compress",
    )(seeds, plan, stash, kv, digits)


def exchanged(value, axis, distance):
    size = lax.axis_size(axis)
    return lax.ppermute(value, axis, [(i, i ^ distance) for i in range(size)])


def split_kernel(axis, keep, got, *outs):
    chips = len(outs)
    rows = keep.shape[0] // chips
    chip = lax.axis_index(axis) // 2
    for step, out in enumerate(outs):
        at = pl.ds(pl.multiple_of((chip ^ step) * rows, rows), rows)
        out[...] = (keep[at, :] + got[at, :].astype(jnp.float32)).astype(out.dtype)


def sum_kernel(*refs):
    *terms, out = refs
    total = terms[0][...]
    for term in terms[1:]:
        total = total + term[...].astype(jnp.float32)
    out[...] = total.astype(out.dtype)


def assemble_kernel(axis, *refs):
    *pieces, out = refs
    chips = len(pieces) // 2
    rows = pieces[0].shape[0]
    device = lax.axis_index(axis)
    for side in range(2):
        core = lax.rem(device, 2) ^ side
        for step in range(chips):
            at = (core * chips + ((device // 2) ^ step)) * rows
            out[pl.ds(pl.multiple_of(at, rows), rows), :] = pieces[side * chips + step][...].astype(out.dtype)


def vmem_call(kernel, outs, name, *args, after=(), cost=None):
    inside, anywhere = pl.BlockSpec(memory_space=pltpu.VMEM), pl.BlockSpec(memory_space=pl.ANY)

    def body(*refs):
        kernel(*refs[:len(args)], *refs[len(args) + len(after):])

    return pl.pallas_call(
        body,
        out_shape=outs,
        in_specs=[inside] * len(args) + [anywhere] * len(after),
        out_specs=jax.tree.map(lambda _: inside, outs),
        compiler_params=pltpu.CompilerParams(vmem_limit_bytes=32 * 2**20),
        cost_estimate=cost,
        name=name,
    )(*args, *after)


def add_kernel(a, b, out):
    out[...] = (a[...].astype(jnp.float32) + b[...].astype(jnp.float32)).astype(out.dtype)


def add_after(a, b, *after):
    return vmem_call(add_kernel, jax.ShapeDtypeStruct(a.shape, a.dtype), "add", a, b, after=after)


def added(a, b):
    return (a.astype(jnp.float32) + b.astype(jnp.float32)).astype(jnp.bfloat16)


def between_places(value, swaps, axis, other_axis):
    size, others = lax.axis_size(axis), lax.axis_size(other_axis)
    goes = dict(swaps) | {b: a for a, b in swaps}
    pairs = [
        (i * size + place, i * size + goes[place] if place in goes else (i ^ 1) * size + place)
        for place in range(size)
        for i in range(others)
    ]
    return lax.ppermute(value, (other_axis, axis), pairs)


def chain(own, axis):
    size, mine = lax.axis_size(axis), lax.axis_index(axis)
    value = own
    for place in range(size - 1, 0, -1):
        got = lax.ppermute(value, axis, [(place, place - 1)])
        value = jnp.where(mine == place - 1, added(got, own), value)
    return value


def per_device(stashed, kv_grads, branch_grads, flora_seeds, plan):
    stash, kv, branch = stashed[0], kv_grads[0], branch_grads[0]
    size = lax.axis_size("dp")
    chips = size // 2
    columns = kv.shape[2]
    if size != 2 * chips or chips not in (1, 2, 4) or lax.axis_size("pipe") != 4:
        kept, _ = compressed_parts(stash, kv, flora_seeds, plan, 1, "dp")
        return lax.psum(kept_part(kept, kv), "dp")[None], chain(branch, "pipe")[None]

    mine = lax.axis_index("pipe")
    rows = branch.shape[0] // 2
    first, second = branch[:rows], branch[rows:]
    pairwise, middle, across = ((3, 2), (1, 0)), ((2, 1),), ((2, 0),)

    def moved(value, swaps):
        return between_places(value, swaps, "pipe", "dp")

    first_a = moved(first, pairwise)
    second_a = moved(second, pairwise)
    kept, send = compressed_parts(stash, kv, flora_seeds, plan, 2, "dp")
    got = exchanged(send, "dp", 1)
    keep = kept_part(kept, kv)
    first_2 = added(first_a, first)
    first_b = moved(first_2, middle)

    piece = (R // size, columns)
    own, *sends = vmem_call(
        functools.partial(split_kernel, "dp"),
        [jax.ShapeDtypeStruct(piece, jnp.float32 if s == 0 else jnp.bfloat16) for s in range(chips)],
        "split", keep, got,
    )
    gots = [exchanged(value, "dp", 2 * s) for s, value in enumerate(sends, 1)]

    second_2 = add_after(second_a, second, keep)
    second_b = moved(second_2, middle)
    second_d = moved(second_2, across)

    done = vmem_call(sum_kernel, jax.ShapeDtypeStruct(piece, jnp.bfloat16), "sum", own, *gots, )
    first_1 = add_after(first_b, first, done)
    first_c = moved(first_1, pairwise)
    here = [done] + [exchanged(done, "dp", 2 * s) for s in range(1, chips)]
    there = [exchanged(value, "dp", 1) for value in here]
    def by_place(values):
        out = values[3]
        for place in range(3):
            out = jnp.where(mine == place, values[place], out)
        return out

    running = jnp.concatenate([
        by_place([added(first_c, first), first_1, first_2, first]),
        by_place([added(added(second_d, second_a), second), added(second_b, second), second_2, second]),
    ])
    compressed = vmem_call(
        functools.partial(assemble_kernel, "dp"), jax.ShapeDtypeStruct((R, columns), jnp.float32),
        "assemble", *here, *there, after=[],
    )

    return compressed[None], running[None]


def solution(mesh):
    placed = (
        P("pipe", None, "dp", None),
        P("pipe", None, "dp", None),
        P("pipe", "dp", None),
        P("pipe", None),
        P("pipe", None),
    )
    return jax.shard_map(
        per_device,
        mesh=mesh,
        in_specs=placed,
        out_specs=(P("pipe", None, None), P("pipe", "dp", None)),
        check_vma=False,
    )
```

```python
import functools
import math

import jax
import jax.numpy as jnp
import ml_dtypes
import numpy as np
from jax import lax
from jax.experimental import pallas as pl
from jax.experimental.pallas import tpu as pltpu
from jax.sharding import PartitionSpec as P

PRIME = 32749
R = 256
TERMS = 32


def balanced(values):
    return (values + PRIME // 2) % PRIME - PRIME // 2


def row_digits(rows):
    r = np.arange(rows, dtype=np.int64)
    a = balanced(1031 * r)
    square = balanced(a * a + 17 * r + 5)
    lines = []
    for factor in (balanced(4 * balanced(square * a)), balanced(4 * a * a + 2 * square), balanced(4 * a)):
        for place in range(3):
            rest = np.floor_divide(factor + 16, 32) if place < 2 else 0 * factor
            lines += [factor - 32 * rest] * 2
            factor = rest
    constant = balanced(square * square - PRIME // 2)
    high = np.floor_divide(constant + 128, 256)
    lines += [np.ones_like(r)] * 2 + [256 * high, constant - 256 * high]
    lines += [np.zeros_like(r)] * (TERMS - len(lines))
    return np.stack(lines).astype(ml_dtypes.bfloat16)


def reduced(values):
    quotient = jnp.round(values.astype(jnp.float32) * jnp.float32(1 / PRIME)).astype(jnp.int32)
    return values - quotient * PRIME


def column_digits(seed, columns):
    c = lax.broadcasted_iota(jnp.int32, (columns, 128), 0)
    term = lax.broadcasted_iota(jnp.int32, (columns, 128), 1)
    b = reduced(2053 * c + (3 * seed + 7))
    b2 = reduced(b * b)
    b3 = reduced(b2 * b)
    added = reduced(reduced(b2 * b2) + 29 * c + seed)
    base = jnp.where(term < 6, b, jnp.where(term < 12, b2, jnp.where(term < 18, b3, added)))
    within = jnp.where(term < 6, term, jnp.where(term < 12, term - 6, term - 12))
    place = jnp.where(term >= 18, 1, jnp.where(within < 2, 1, jnp.where(within < 4, 32, 1024)))
    whole = reduced(base * place).astype(jnp.float32)
    high = jnp.round(whole * (1 / 256)) * 256
    digit = jnp.where((term & 1) == 0, high, whole - high)
    digit = jnp.where(term >= 20, jnp.where(term < 22, 1.0, 0.0), digit)
    return digit.astype(jnp.bfloat16)


def tokens_dot(left, right):
    return lax.dot_general(left, right, (((0,), (0,)), ((), ())), preferred_element_type=jnp.float32)


def compress_kernel(
    tile, groups, scale, halves, axis,
    seeds_hbm, plan_hbm, stash, kv_hbm, digits_hbm, kept, send,
    seeds, plan, x, kv, digits, columns, total, scalar_sem, x_sem, kv_sem, digit_sem,
):
    slots, tokens, width = stash.shape
    span = width // groups
    scalars = [
        pltpu.make_async_copy(seeds_hbm, seeds, scalar_sem.at[0]),
        pltpu.make_async_copy(plan_hbm, plan, scalar_sem.at[1]),
    ]
    digit_copy = pltpu.make_async_copy(digits_hbm, digits, digit_sem)
    copies = [
        pltpu.make_async_copy(
            stash.at[:, :, pl.ds(g * span, span)], x.at[:, :, pl.ds(g * span, span)], x_sem.at[g]
        )
        for g in range(groups)
    ]
    kv_copy = pltpu.make_async_copy(kv_hbm, kv, kv_sem)
    for copy in (*scalars, digit_copy, *copies, kv_copy):
        copy.start()
    for copy in scalars:
        copy.wait()
    columns[0:R, :] = column_digits(seeds[0, 0], R)
    columns[R:, :] = column_digits(seeds[0, 1], R)
    digit_copy.wait()
    total[...] = jnp.zeros_like(total)
    for g in range(groups):
        copies[g].wait()
        for i in range(span // tile):
            part = pl.ds(g * span + i * tile, tile)
            hashed = jnp.dot(columns[:, 0:TERMS], digits[:, part], preferred_element_type=jnp.float32)
            turns = hashed * jnp.float32(1 / PRIME)
            proj = ((turns - jnp.round(turns)) * jnp.float32(scale)).astype(jnp.bfloat16)
            total[...] += lax.dot_general(
                x[:, :, part].reshape(slots * tokens, tile), proj, (((1,), (1,)), ((), ())),
                preferred_element_type=jnp.float32,
            )
    count = slots * tokens
    slot_row = lax.broadcasted_iota(jnp.int32, (count, count), 0)
    place = slot_row
    for k in range(slots):
        within = (slot_row >= k * tokens) & (slot_row < (k + 1) * tokens)
        place = jnp.where(within, slot_row + (plan[0, k] - k) * tokens, place)
    moves = (place == lax.broadcasted_iota(jnp.int32, (count, count), 1)).astype(jnp.bfloat16)
    total[...] = tokens_dot(moves, total[...].astype(jnp.bfloat16))
    kv_copy.wait()
    half = kv.shape[2] // 2
    targets = kv[...].reshape(slots * tokens, 2 * half)
    rows = R // halves
    mine = lax.rem(lax.axis_index(axis), halves)
    for side in range(2):
        kept[side] = total[:, pl.ds(pl.multiple_of(side * R + mine * rows, rows), rows)].astype(jnp.bfloat16)
        if halves > 1:
            other = pl.multiple_of(side * R + (1 - mine) * rows, rows)
            left = total[:, pl.ds(other, rows)].astype(jnp.bfloat16)
            cols = slice(side * half, (side + 1) * half)
            send[:, cols] = tokens_dot(left, targets[:, cols]).astype(send.dtype)


def keep_kernel(kept, kv, out):
    slots, tokens, width = kv.shape
    targets = kv[...].reshape(slots * tokens, width)
    for side in range(2):
        cols = slice(side * width // 2, (side + 1) * width // 2)
        out[:, cols] = tokens_dot(kept[side], targets[:, cols])


def kept_part(kept, kv):
    out = jax.ShapeDtypeStruct((kept.shape[2], kv.shape[2]), jnp.float32)
    return vmem_call(keep_kernel, out, "keep", kept, kv)


def compressed_parts(stash, kv, seeds, plan, halves, axis):
    slots, tokens, width = stash.shape
    groups = 2
    tile = width // 8
    scale = PRIME * 2.0 / (PRIME - 1) * math.sqrt(3.0 / width)
    far = pl.BlockSpec(memory_space=pl.ANY)
    digits = jnp.asarray(row_digits(width))
    part = (R // halves, kv.shape[2])
    sides = (2, slots * tokens, R // halves)
    return pl.pallas_call(
        functools.partial(compress_kernel, tile, groups, scale, halves, axis),
        out_shape=[jax.ShapeDtypeStruct(sides, jnp.bfloat16), jax.ShapeDtypeStruct(part, jnp.bfloat16)],
        in_specs=[far] * 5,
        out_specs=[pl.BlockSpec(memory_space=pltpu.VMEM)] * 2,
        scratch_shapes=[
            pltpu.SMEM(seeds.shape, jnp.int32),
            pltpu.SMEM(plan.shape, jnp.int32),
            pltpu.VMEM((slots, tokens, width), jnp.bfloat16),
            pltpu.VMEM(kv.shape, jnp.bfloat16),
            pltpu.VMEM(digits.shape, jnp.bfloat16),
            pltpu.VMEM((2 * R, 128), jnp.bfloat16),
            pltpu.VMEM((slots * tokens, 2 * R), jnp.float32),
            pltpu.SemaphoreType.DMA((2,)),
            pltpu.SemaphoreType.DMA((groups,)),
            pltpu.SemaphoreType.DMA,
            pltpu.SemaphoreType.DMA,
        ],
        compiler_params=pltpu.CompilerParams(vmem_limit_bytes=60 * 2**20),
        cost_estimate=pl.CostEstimate(flops=8 * 10**9, bytes_accessed=28 * 10**6, transcendentals=0),
        name="compress",
    )(seeds, plan, stash, kv, digits)


def exchanged(value, axis, distance):
    size = lax.axis_size(axis)
    return lax.ppermute(value, axis, [(i, i ^ distance) for i in range(size)])


def split_kernel(axis, keep, got, *outs):
    chips = len(outs)
    rows = keep.shape[0] // chips
    chip = lax.axis_index(axis) // 2
    for step, out in enumerate(outs):
        at = pl.ds(pl.multiple_of((chip ^ step) * rows, rows), rows)
        out[...] = (keep[at, :] + got[at, :].astype(jnp.float32)).astype(out.dtype)


def sum_kernel(*refs):
    *terms, out = refs
    total = terms[0][...]
    for term in terms[1:]:
        total = total + term[...].astype(jnp.float32)
    out[...] = total.astype(out.dtype)


def placed(blocks, at, out, before=None):
    inside, anywhere = pl.BlockSpec(memory_space=pltpu.VMEM), pl.BlockSpec(memory_space=pl.ANY)
    counts = [len(operands) for _, operands in blocks]
    operands = [operand for _, group in blocks for operand in group]
    earlier = [] if before is None else [before]
    rows = [group[0].shape[0] for _, group in blocks]

    def body(*refs):
        ins, target = refs[:len(operands)], refs[len(operands) + len(earlier)]
        scratch, sems = refs[len(operands) + len(earlier) + 1:-1], refs[-1]
        copies, start = [], 0
        for index, (make, _) in enumerate(blocks):
            scratch[index][...] = make(*ins[start:start + counts[index]])
            start += counts[index]
            to = target.at[pl.ds(pl.multiple_of(at(index), rows[index]), rows[index])]
            copies.append(pltpu.make_async_copy(scratch[index], to, sems.at[index]))
            copies[-1].start()
        for copy in copies:
            copy.wait()

    return pl.pallas_call(
        body,
        out_shape=out,
        in_specs=[inside] * len(operands) + [anywhere] * len(earlier),
        out_specs=anywhere,
        scratch_shapes=[
            *(pltpu.VMEM((count, *out.shape[1:]), out.dtype) for count in rows),
            pltpu.SemaphoreType.DMA((len(blocks),)),
        ],
        input_output_aliases={len(operands): 0} if earlier else {},
        compiler_params=pltpu.CompilerParams(vmem_limit_bytes=32 * 2**20),
        name="place",
    )(*operands, *earlier)


def widened(ref):
    return ref[...].astype(jnp.float32)


def vmem_call(kernel, outs, name, *args, after=(), cost=None):
    inside, anywhere = pl.BlockSpec(memory_space=pltpu.VMEM), pl.BlockSpec(memory_space=pl.ANY)

    def body(*refs):
        kernel(*refs[:len(args)], *refs[len(args) + len(after):])

    return pl.pallas_call(
        body,
        out_shape=outs,
        in_specs=[inside] * len(args) + [anywhere] * len(after),
        out_specs=jax.tree.map(lambda _: inside, outs),
        compiler_params=pltpu.CompilerParams(vmem_limit_bytes=32 * 2**20),
        cost_estimate=cost,
        name=name,
    )(*args, *after)


def add_kernel(a, b, out):
    out[...] = (a[...].astype(jnp.float32) + b[...].astype(jnp.float32)).astype(out.dtype)


def add_after(a, b, *after):
    return vmem_call(add_kernel, jax.ShapeDtypeStruct(a.shape, a.dtype), "add", a, b, after=after)


def added(a, b):
    return (a.astype(jnp.float32) + b.astype(jnp.float32)).astype(jnp.bfloat16)


def between_places(value, swaps, axis, other_axis):
    size, others = lax.axis_size(axis), lax.axis_size(other_axis)
    goes = dict(swaps) | {b: a for a, b in swaps}
    pairs = [
        (i * size + place, i * size + goes[place] if place in goes else (i ^ 1) * size + place)
        for place in range(size)
        for i in range(others)
    ]
    return lax.ppermute(value, (other_axis, axis), pairs)


def chain(own, axis):
    size, mine = lax.axis_size(axis), lax.axis_index(axis)
    value = own
    for place in range(size - 1, 0, -1):
        got = lax.ppermute(value, axis, [(place, place - 1)])
        value = jnp.where(mine == place - 1, added(got, own), value)
    return value


def per_device(stashed, kv_grads, branch_grads, flora_seeds, plan):
    stash, kv, branch = stashed[0], kv_grads[0], branch_grads[0]
    size = lax.axis_size("dp")
    chips = size // 2
    columns = kv.shape[2]
    if size != 2 * chips or chips not in (1, 2, 4) or lax.axis_size("pipe") != 4:
        kept, _ = compressed_parts(stash, kv, flora_seeds, plan, 1, "dp")
        return lax.psum(kept_part(kept, kv), "dp")[None], chain(branch, "pipe")[None]

    rows = branch.shape[0] // 2
    first, second = branch[:rows], branch[rows:]
    pairwise, middle, across = ((3, 2), (1, 0)), ((2, 1),), ((2, 0),)

    def moved(value, swaps):
        return between_places(value, swaps, "pipe", "dp")

    first_a = moved(first, pairwise)
    second_a = moved(second, pairwise)
    kept, send = compressed_parts(stash, kv, flora_seeds, plan, 2, "dp")
    got = exchanged(send, "dp", 1)
    keep = kept_part(kept, kv)
    first_2 = added(first_a, first)
    first_b = moved(first_2, middle)

    piece = (R // size, columns)
    own, *sends = vmem_call(
        functools.partial(split_kernel, "dp"),
        [jax.ShapeDtypeStruct(piece, jnp.float32 if s == 0 else jnp.bfloat16) for s in range(chips)],
        "split", keep, got,
    )
    gots = [exchanged(value, "dp", 2 * s) for s, value in enumerate(sends, 1)]

    second_2 = add_after(second_a, second, keep)
    second_b = moved(second_2, middle)
    second_d = moved(second_2, across)

    done = vmem_call(sum_kernel, jax.ShapeDtypeStruct(piece, jnp.bfloat16), "sum", own, *gots, )
    first_1 = add_after(first_b, first, done)
    first_c = moved(first_1, pairwise)
    here = [done] + [exchanged(done, "dp", 2 * s) for s in range(1, chips)]
    there = [exchanged(value, "dp", 1) for value in here]
    def at_rows(steps):
        def at(index):
            side, step = steps[index]
            device = lax.axis_index("dp")
            return ((lax.rem(device, 2) ^ side) * chips + ((device // 2) ^ step)) * piece[0]
        return at

    whole = jax.ShapeDtypeStruct((R, columns), jnp.float32)
    early = [(side, step) for step in range(chips) for side in range(2)]
    late = []
    pieces = (here, there)
    compressed = placed([(widened, [pieces[a][b]]) for a, b in early], at_rows(early), whole)
    if late:
        compressed = placed([(widened, [pieces[a][b]]) for a, b in late], at_rows(late), whole, compressed)

    def by_place(values):
        out = values[3]
        for place in range(3):
            out = jnp.where(lax.axis_index("pipe") == place, values[place], out)
        return out

    running = jnp.concatenate([
        by_place([added(first_c, first), first_1, first_2, first]),
        by_place([added(added(second_d, second_a), second), added(second_b, second), second_2, second]),
    ])
    return compressed[None], running[None]


def solution(mesh):
    placed = (
        P("pipe", None, "dp", None),
        P("pipe", None, "dp", None),
        P("pipe", "dp", None),
        P("pipe", None),
        P("pipe", None),
    )
    return jax.shard_map(
        per_device,
        mesh=mesh,
        in_specs=placed,
        out_specs=(P("pipe", None, None), P("pipe", "dp", None)),
        check_vma=False,
    )
```
